512 devices in a mesh: dp: 32 (over z, x), tensor: 16 (over y, core).
Axes of the slice: x: 4, y: 8, z: 8, core: 2. Of those that a mesh axis runs over, the one named last changes fastest.
Arguments:
- queries: bfloat16 [512, 256, 4096], P('dp', None, 'tensor'), may hold values from -250 to 250
- keys_values: bfloat16 [512, 256, 2, 512], P('dp', 'tensor'), may hold values from -50 to 50
- donors: int32 [512, 16], replicated, may hold values from 0 to 511, as said below
- ablated: int32 [16], replicated, may hold values from 0 to 31, as said below
Outputs:
- patched: bfloat16 [512, 256, 4096], P('dp', None, 'tensor')
The draws below stay inside these ranges and needn't reach their ends.
Inputs may be any that keep to these rules, and one draw needn't show every extreme that they name: `ablated`: entry k lies among heads 2 * k to 2 * k + 1. For each column and each aligned block of 16 prompts, at most 1 of its donors lie in any one aligned block of 16 prompts, and exactly 1 in some.
All inputs are finite; a program needn't handle non-finite values.
Results may differ from the reference program's by a relative error of at most 0.0046.
Values may be sent and summed in bfloat16 or wider, within the bound.
A program may use at most 64 MiB of HBM per device.

```python
import math
import jax
import jax.numpy as jnp
from jax import lax

HSIZE = 128
HEAD_DEV = 2
GROUP = 8
SEQ = 256
PR_DEV = 16
PROMPTS = 512
CAP = 1
HEADS = 32
KVH = 4
ABL = 16


def shared_keys(key):
    drawn = jax.random.normal(jax.random.fold_in(key, 101), (PROMPTS, SEQ, KVH, HSIZE), jnp.float32)
    return jnp.clip(drawn, -5.0, 5.0)


def draw_queries(key, part):
    key = jax.random.fold_in(key, 3)
    drawn = jnp.clip(jax.random.normal(key, (PROMPTS, SEQ, HEADS, HSIZE), jnp.float32), -5.0, 5.0)
    return drawn.reshape(PROMPTS, SEQ, HEADS * HSIZE).astype(jnp.bfloat16)


def draw_keys_values(key, part):
    base_keys = shared_keys(key)
    key = jax.random.fold_in(key, 5)
    key_part = base_keys
    value_part = jnp.clip(jax.random.normal(key, (PROMPTS, SEQ, KVH, HSIZE), jnp.float32), -5.0, 5.0)
    stacked = jnp.stack([key_part, value_part], axis=2)
    return stacked.reshape(PROMPTS, SEQ, 2, KVH * HSIZE).astype(jnp.bfloat16)


def draw_donors(key, part):
    key = jax.random.fold_in(key, 11)
    n_dev = PROMPTS // PR_DEV
    copies = n_dev * CAP
    rank_bits = jax.random.randint(jax.random.fold_in(key, 1), (ABL, n_dev), 0, 2 ** 20) * n_dev + jnp.arange(n_dev)
    rank_table = jnp.argsort(rank_bits, axis=1)
    popular = (rank_table < max(n_dev // 4, 1)).astype(jnp.int32)
    popular_copies = jnp.repeat(popular, CAP, axis=1)
    noise_bits = jax.random.randint(jax.random.fold_in(key, 2), (n_dev, ABL, copies), 0, 1024)
    scores = (noise_bits + popular_copies[None] * 512) * copies + jnp.arange(copies)
    unused, picked = lax.top_k(scores, PR_DEV)
    sources = picked // CAP
    shuffle_bits = jax.random.randint(jax.random.fold_in(key, 3), (n_dev, ABL, PR_DEV), 0, 1024) * PR_DEV + jnp.arange(PR_DEV)
    reorder = jnp.argsort(shuffle_bits, axis=2)
    sources = jnp.take_along_axis(sources, reorder, axis=2)
    offset_rows = jax.random.randint(jax.random.fold_in(key, 4), (n_dev, ABL, PR_DEV), 0, PR_DEV)
    donor_table = sources * PR_DEV + offset_rows
    return jnp.transpose(donor_table, (0, 2, 1)).reshape(PROMPTS, ABL).astype(jnp.int32)


def draw_ablated(key, part):
    key = jax.random.fold_in(key, 13)
    offsets = jax.random.randint(key, (ABL,), 0, HEAD_DEV)
    return (jnp.arange(ABL) * HEAD_DEV + offsets).astype(jnp.int32)


def setup_inputs(seed: int = 0) -> dict:
    streams_of = jax.random.split(jax.random.key(seed), 5)
    queries = draw_queries(jax.random.fold_in(streams_of[4], 71), 0)
    keys_values = draw_keys_values(jax.random.fold_in(streams_of[4], 71), 0)
    donors = draw_donors(jax.random.fold_in(streams_of[4], 71), 0)
    ablated = draw_ablated(jax.random.fold_in(streams_of[4], 71), 0)
    return {"queries": queries, "keys_values": keys_values, "donors": donors, "ablated": ablated}


def one_prompt(inputs):
    head_rows, key_value = inputs
    length = head_rows.shape[0]
    key_rows = jnp.repeat(key_value[:, 0], GROUP, axis=1).astype(jnp.float32)
    value_rows = jnp.repeat(key_value[:, 1], GROUP, axis=1).astype(jnp.float32)
    scores = jnp.einsum('shd,thd->hst', head_rows.astype(jnp.float32), key_rows) * (1.0 / math.sqrt(HSIZE))
    causal = lax.broadcasted_iota(jnp.int32, (length, length), 0) >= lax.broadcasted_iota(jnp.int32, (length, length), 1)
    scores = jnp.where(causal[None], scores, -jnp.inf)
    row_max = lax.optimization_barrier(jnp.max(scores, axis=2, keepdims=True))
    powers = jnp.exp(scores - row_max)
    weights = (powers / lax.optimization_barrier(jnp.sum(powers, axis=2, keepdims=True))).astype(jnp.bfloat16)
    return jnp.einsum('hst,thd->shd', weights.astype(jnp.float32), value_rows).astype(jnp.bfloat16)

def reference(queries, keys_values, donors, ablated):
    prompts, length, row_width = queries.shape
    per_head = queries.reshape(prompts, length, HEADS, HSIZE)
    key_value = keys_values.reshape(prompts, length, 2, KVH, HSIZE)
    outputs = lax.map(one_prompt, (per_head, key_value))
    patched = outputs
    for slot_index in range(ABL):
        head_index = ablated[slot_index]
        column = lax.dynamic_index_in_dim(outputs, head_index, 2, keepdims=False)
        donated = jnp.take(column, donors[:, slot_index], axis=0)
        patched = lax.dynamic_update_index_in_dim(patched, donated, head_index, 2)
    return patched.reshape(prompts, length, row_width)
```

```python
import functools
import math

import jax
import jax.numpy as jnp
from jax import lax
from jax.experimental import pallas as pl
from jax.experimental.pallas import tpu as pltpu
from jax.sharding import PartitionSpec as P

MESH = pl.DeviceIdType.MESH
HSIZE = 128
PROMPTS_DEV = 16
SEQ = 256
NZ, NX, NY = 8, 4, 8
NDP = NZ * NX
PIECE = 16
CHUNK = 32
LAST = 2 * NY
RATE = math.log2(math.e) / math.sqrt(HSIZE)


def attend(query_rows, key_rows, value_rows, first):
    scores = lax.dot_general(
        query_rows, key_rows, (((1,), (1,)), ((), ())), preferred_element_type=jnp.float32
    )
    rows = lax.broadcasted_iota(jnp.int32, scores.shape, 0) + first
    columns = lax.broadcasted_iota(jnp.int32, scores.shape, 1)
    scores = jnp.where(rows >= columns, scores, -jnp.inf)
    row_max = jnp.max(scores, axis=1, keepdims=True)
    powers = jnp.exp2((scores - row_max) * RATE)
    weights = (powers * (1.0 / jnp.sum(powers, axis=1, keepdims=True))).astype(jnp.bfloat16)
    return jnp.dot(weights, value_rows, preferred_element_type=jnp.float32).astype(jnp.bfloat16)


def kernel(
    q_ref, kv_ref, donors_ref, ablated_ref, out_ref,
    q_buf, kv_buf, own_buf, send_buf, recv_buf, row_tab,
    q_sem, own_sem, first_send, near_send, twin_send, kv_recv, dp_send, dp_recv,
):
    dp = lax.axis_index("dp")
    tensor = lax.axis_index("tensor")
    z, x = dp // NX, dp % NX
    y, core = tensor // 2, tensor % 2
    group = y // 2
    sign = 1 - 2 * (y % 2)
    near = y + sign
    twin = 1 - core

    def in_group(chip, c):
        return (dp, (chip + 2 * NY) % NY * 2 + c)

    def partner(slot, direction):
        to_z = (z + direction * (slot // NX) + NZ) % NZ
        to_x = (x + direction * (slot % NX) + NX) % NX
        return (to_z * NX + to_x, tensor)

    barrier = pltpu.get_barrier_semaphore()
    for target in [in_group(y - sign * i, core) for i in (1, 2, 3)] + [in_group(near, core), in_group(y, twin)]:
        pl.semaphore_signal(barrier, inc=1, device_id=target, device_id_type=MESH)

    def greet(slot, carry):
        pl.semaphore_signal(barrier, inc=1, device_id=partner(slot, -1), device_id_type=MESH)
        return carry

    lax.fori_loop(1, NDP, greet, 0)

    q_copies = [
        pltpu.make_async_copy(q_ref.at[:, :, pl.ds(i * HSIZE, HSIZE)], q_buf.at[i], q_sem.at[i])
        for i in range(2)
    ]
    for copy in q_copies:
        copy.start()
    own_copy = pltpu.make_async_copy(kv_ref.at[group], kv_buf.at[tensor], own_sem)
    own_copy.start()

    head = ablated_ref[tensor] % 2

    def find_row(slot, carry):
        dest = ((z + slot // NX) % NZ) * NX + (x + slot % NX) % NX
        row = 0
        for p in range(PROMPTS_DEV):
            donor = donors_ref[tensor, dest * PROMPTS_DEV + p]
            row = row + jnp.where(donor // PROMPTS_DEV == dp, donor % PROMPTS_DEV, 0)
        row_tab[slot] = row
        return carry

    lax.fori_loop(0, NDP, find_row, 0)

    pl.semaphore_wait(barrier, NDP - 1 + 5)

    first_copies = []
    for i, step in enumerate((-1, 2, -3)):
        chip = (y + sign * step + 2 * NY) % NY
        first_copies.append(
            pltpu.make_async_remote_copy(
                src_ref=kv_ref.at[chip // 2],
                dst_ref=kv_buf.at[tensor],
                send_sem=first_send.at[i],
                recv_sem=kv_recv.at[tensor],
                device_id=in_group(chip, core),
                device_id_type=MESH,
            )
        )

    def forward(piece, sem, target):
        return pltpu.make_async_remote_copy(
            src_ref=kv_buf.at[piece],
            dst_ref=kv_buf.at[piece],
            send_sem=sem,
            recv_sem=kv_recv.at[piece],
            device_id=target,
            device_id_type=MESH,
        )

    def near_copy(ch):
        return forward(2 * ch + core, near_send.at[ch], in_group(near, core))

    def twin_copy(ch):
        return forward(2 * ch + core, twin_send.at[ch], in_group(y, twin))

    def place(ch):
        return (sign * (y - ch) + 2 * NY) % NY

    for copy in first_copies:
        copy.start()
    own_copy.wait()

    def head_rows(p, start, size, which):
        return q_buf[which, p, start : start + size]

    def keys_of(p, part, length):
        return kv_buf[0 : length // PIECE, part, p].reshape(length, HSIZE)

    for ch in range(NY):
        start, length = ch * CHUNK, (ch + 1) * CHUNK

        @pl.when(place(ch) != 0)
        def _():
            forward(2 * ch + core, near_send.at[ch], in_group(near, core)).wait_recv()

        @pl.when(place(ch) < 4)
        def _():
            near_copy(ch).start()

        twin_copy(ch).start()
        forward(2 * ch + twin, twin_send.at[ch], in_group(y, twin)).wait_recv()
        if ch == 0:
            for copy in q_copies:
                copy.wait()

        def one_prompt(p, carry):
            own_buf[p, start:length] = attend(
                head_rows(p, start, CHUNK, head), keys_of(p, 0, length), keys_of(p, 1, length), start
            )
            return carry

        lax.fori_loop(0, PROMPTS_DEV, one_prompt, 0, unroll=4)

        recv_buf[0, start:length] = own_buf[row_tab[0], start:length]

        def send(slot, carry):
            send_buf[slot, start:length] = own_buf[row_tab[slot], start:length]
            pltpu.make_async_remote_copy(
                src_ref=send_buf.at[slot, pl.ds(start, CHUNK)],
                dst_ref=recv_buf.at[slot, pl.ds(start, CHUNK)],
                send_sem=dp_send,
                recv_sem=dp_recv,
                device_id=partner(slot, 1),
                device_id_type=MESH,
            ).start()
            return carry

        lax.fori_loop(1, NDP, send, 0)

    for copy in first_copies:
        copy.wait_send()
    for ch in range(NY):
        twin_copy(ch).wait_send()

        @pl.when(place(ch) < 4)
        def _():
            near_copy(ch).wait_send()

    half = SEQ // 2

    def other_head(p, carry):
        for start in (0, half):
            length = start + half
            rows = attend(
                head_rows(p, start, half, 1 - head), keys_of(p, 0, length), keys_of(p, 1, length), start
            )
            out_ref[p, start:length, 0:HSIZE] = rows
            out_ref[p, start:length, HSIZE:] = rows
        return carry

    lax.fori_loop(0, PROMPTS_DEV, other_head, 0)

    everything = pltpu.make_async_remote_copy(
        src_ref=send_buf.at[pl.ds(1, NDP - 1)],
        dst_ref=recv_buf.at[pl.ds(1, NDP - 1)],
        send_sem=dp_send,
        recv_sem=dp_recv,
        device_id=partner(1, 1),
        device_id_type=MESH,
    )
    everything.wait()

    def patch(p, carry):
        source = donors_ref[tensor, dp * PROMPTS_DEV + p] // PROMPTS_DEV
        slot = ((z - source // NX + NZ) % NZ) * NX + (x - source % NX + NX) % NX
        block = recv_buf[slot]
        lower = jnp.full(block.shape, head, jnp.int32) == 0
        out_ref[p, :, 0:HSIZE] = jnp.where(lower, block, out_ref[p, :, 0:HSIZE])
        out_ref[p, :, HSIZE:] = jnp.where(lower, out_ref[p, :, HSIZE:], block)
        return carry

    lax.fori_loop(0, PROMPTS_DEV, patch, 0)


def on_device(queries, keys_values, donors, ablated):
    prompts, length, width = queries.shape
    pieces = keys_values.reshape(prompts, PIECE, 2, 4, HSIZE).transpose(3, 2, 0, 1, 4)
    anywhere = pl.BlockSpec(memory_space=pl.ANY)
    scalars = pl.BlockSpec(memory_space=pltpu.SMEM)
    dma = pltpu.SemaphoreType.DMA
    return pl.pallas_call(
        kernel,
        out_shape=jax.ShapeDtypeStruct(queries.shape, jnp.bfloat16),
        in_specs=[anywhere, anywhere, scalars, scalars],
        out_specs=pl.BlockSpec(memory_space=pltpu.VMEM),
        scratch_shapes=[
            pltpu.VMEM((2, prompts, length, HSIZE), jnp.bfloat16),
            pltpu.VMEM((LAST, 2, prompts, PIECE, HSIZE), jnp.bfloat16),
            pltpu.VMEM((prompts, length, HSIZE), jnp.bfloat16),
            pltpu.VMEM((NDP, length, HSIZE), jnp.bfloat16),
            pltpu.VMEM((NDP, length, HSIZE), jnp.bfloat16),
            pltpu.SMEM((NDP,), jnp.int32),
            dma((2,)), dma, dma((3,)), dma((NY,)), dma((NY,)), dma((LAST,)), dma, dma,
        ],
        compiler_params=pltpu.CompilerParams(
            collective_id=0, has_side_effects=True, vmem_limit_bytes=40 * 2**20
        ),
    )(queries, pieces, donors.T, ablated)


def solution(mesh):
    return jax.shard_map(
        on_device,
        mesh=mesh,
        in_specs=(P("dp", None, "tensor"), P("dp", "tensor", None, None), P(), P()),
        out_specs=P("dp", None, "tensor"),
        check_vma=False,
    )
```

```python
import functools
import math

import jax
import jax.numpy as jnp
from jax import lax
from jax.experimental import pallas as pl
from jax.experimental.pallas import tpu as pltpu
from jax.sharding import PartitionSpec as P

MESH = pl.DeviceIdType.MESH
HSIZE = 128
PROMPTS_DEV = 16
SEQ = 256
NZ, NX, NY = 8, 4, 8
NDP = NZ * NX
PIECE = 16
CHIP = 2 * PIECE
CHUNKS = ((0, 64, 4), (64, 128, 4), (128, 256, 2))
WAVES = ((0, 4), (4, 8))
LAST = 2 * NY
RATE = math.log2(math.e) / math.sqrt(HSIZE)


def attend(query_rows, key_rows, value_rows, first):
    scores = lax.dot_general(
        query_rows, key_rows, (((1,), (1,)), ((), ())), preferred_element_type=jnp.float32
    )
    rows = lax.broadcasted_iota(jnp.int32, scores.shape, 0) + first
    columns = lax.broadcasted_iota(jnp.int32, scores.shape, 1)
    scores = jnp.where(rows >= columns, scores, -jnp.inf)
    row_max = jnp.max(scores, axis=1, keepdims=True)
    powers = jnp.exp2((scores - row_max) * RATE)
    weights = (powers * (1.0 / jnp.sum(powers, axis=1, keepdims=True))).astype(jnp.bfloat16)
    return jnp.dot(weights, value_rows, preferred_element_type=jnp.float32).astype(jnp.bfloat16)


def kernel(
    q_ref, kv_ref, donors_hbm, ablated_ref, out_ref,
    q_buf, kv_buf, own_buf, send_buf, recv_bufs, donors_ref, row_tab, slot_tab,
    q_sem, own_sem, table_sem, first_send, near_send, twin_send, kv_recv, dp_send, dp_recv,
):
    dp = lax.axis_index("dp")
    tensor = lax.axis_index("tensor")
    z, x = lax.div(dp, NX), lax.rem(dp, NX)
    y, core = lax.div(tensor, 2), lax.rem(tensor, 2)
    group = lax.div(y, 2)
    sign = 1 - 2 * lax.rem(y, 2)
    near = y + sign
    twin = 1 - core

    def in_group(chip, c):
        return (dp, lax.rem(chip + 2 * NY, NY) * 2 + c)

    def shifted(slot, direction):
        to_z = lax.rem(z + direction * lax.div(slot, NX) + NZ, NZ)
        to_x = lax.rem(x + direction * lax.rem(slot, NX) + NX, NX)
        return to_z * NX + to_x

    barrier = pltpu.get_barrier_semaphore()
    for target in [in_group(y - sign * i, core) for i in (1, 2, 3)] + [in_group(near, core), in_group(y, twin)]:
        pl.semaphore_signal(barrier, inc=1, device_id=target, device_id_type=MESH)

    def greet(slot, carry):
        pl.semaphore_signal(barrier, inc=1, device_id=(shifted(slot, -1), tensor), device_id_type=MESH)
        return carry

    lax.fori_loop(1, NDP, greet, 0)

    q_copies = [
        pltpu.make_async_copy(q_ref.at[:, :, pl.ds(i * HSIZE, HSIZE)], q_buf.at[i], q_sem.at[i])
        for i in range(2)
    ]
    for copy in q_copies:
        copy.start()
    own_copy = pltpu.make_async_copy(kv_ref.at[group], kv_buf.at[tensor], own_sem)
    own_copy.start()
    table_copy = pltpu.make_async_copy(donors_hbm, donors_ref, table_sem)
    table_copy.start()

    pl.semaphore_wait(barrier, NDP - 1 + 5)

    def first_copies():
        copies = []
        for i, step in enumerate((-1, 2, -3)):
            chip = lax.rem(y + sign * step + 2 * NY, NY)
            copies.append(
                pltpu.make_async_remote_copy(
                    src_ref=kv_ref.at[lax.div(chip, 2)],
                    dst_ref=kv_buf.at[tensor],
                    send_sem=first_send.at[i],
                    recv_sem=kv_recv.at[tensor],
                    device_id=in_group(chip, core),
                    device_id_type=MESH,
                )
            )
        return copies

    def forward(source, piece, sem, target):
        return pltpu.make_async_remote_copy(
            src_ref=source,
            dst_ref=kv_buf.at[piece],
            send_sem=sem,
            recv_sem=kv_recv.at[piece],
            device_id=target,
            device_id_type=MESH,
        )

    def handled(i):
        return lax.rem(y - sign * i + 2 * NY, NY)

    def passed(i):
        return lax.rem(near + sign * i + 2 * NY, NY)

    def near_copy(i, source):
        return forward(source, 2 * handled(i) + core, near_send.at[i], in_group(near, core))

    def twin_copy(ch, source):
        return forward(source, 2 * ch + core, twin_send.at[ch], in_group(y, twin))

    def take(i):
        ch = handled(i)
        piece = kv_buf.at[2 * ch + core]
        near_copy(i, piece).wait_recv()
        near_copy(i, piece).start()
        twin_copy(ch, piece).start()

    def take_passed(i):
        ch = passed(i)
        piece = kv_buf.at[2 * ch + core]
        twin_copy(ch, piece).wait_recv()
        twin_copy(ch, piece).start()

    def when_in(chips, ch, action, *values):
        first, last = chips
        pl.when(jnp.logical_and(ch >= first, ch < last))(lambda: action(*values))

    def start_own():
        for copy in [near_copy(0, kv_ref.at[group]), twin_copy(y, kv_ref.at[group])] + first_copies():
            copy.start()

    def pass_on(chips):
        when_in(chips, passed(0), take_passed, 0)
        for i in (1, 2, 3):
            when_in(chips, handled(i), take, i)
            when_in(chips, passed(i), take_passed, i)

    def arrive(chips):
        for ch in range(*chips):
            piece = 2 * ch + twin
            forward(kv_buf.at[piece], piece, twin_send.at[ch], in_group(y, twin)).wait_recv()

    start_own()
    own_copy.wait()

    table_copy.wait()
    head = lax.rem(ablated_ref[tensor], 2)

    def find_row(slot, carry):
        dest = shifted(slot, 1)
        row = 0
        for p in range(PROMPTS_DEV):
            donor = donors_ref[tensor, dest * PROMPTS_DEV + p]
            row = row + jnp.where(lax.div(donor, PROMPTS_DEV) == dp, lax.rem(donor, PROMPTS_DEV), 0)
        row_tab[slot] = row
        return carry

    lax.fori_loop(0, NDP, find_row, 0)

    def find_slot(p, carry):
        source = lax.div(donors_ref[tensor, dp * PROMPTS_DEV + p], PROMPTS_DEV)
        slot_z = lax.rem(z - lax.div(source, NX) + NZ, NZ)
        slot_tab[p] = slot_z * NX + lax.rem(x - lax.rem(source, NX) + NX, NX)
        return carry

    lax.fori_loop(0, PROMPTS_DEV, find_slot, 0)

    def keys_of(p, part, length):
        return kv_buf[0 : length // PIECE, part, p].reshape(length, HSIZE)

    def ablated_chunk(start, length, batch):
        def prompts(i, carry):
            results = []
            for j in range(batch):
                p = i * batch + j
                results.append(
                    attend(q_buf[head, p, start:length], keys_of(p, 0, length), keys_of(p, 1, length), start)
                )
            for j in range(batch):
                own_buf[i * batch + j, start:length] = results[j]
            return carry

        lax.fori_loop(0, PROMPTS_DEV // batch, prompts, 0)

    def send_chunk(c, start, length):
        size = length - start
        recv_bufs[c][0] = own_buf[row_tab[0], start:length]

        def send(slot, carry):
            block = pl.ds(NDP * start + slot * size, size)
            send_buf[block] = own_buf[row_tab[slot], start:length]
            pltpu.make_async_remote_copy(
                src_ref=send_buf.at[block],
                dst_ref=recv_bufs[c].at[slot],
                send_sem=dp_send.at[c],
                recv_sem=dp_recv.at[c],
                device_id=(shifted(slot, 1), tensor),
                device_id_type=MESH,
            ).start()
            return carry

        lax.fori_loop(1, NDP, send, 0)

    for c, (start, length, batch) in enumerate(CHUNKS):
        wave = [w for w in range(len(WAVES)) if WAVES[w][0] * CHIP == start]
        for w in wave:
            pass_on(WAVES[w])
            arrive(WAVES[w])
        if c == 0:
            for copy in q_copies:
                copy.wait()
        ablated_chunk(start, length, batch)
        send_chunk(c, start, length)

    half = SEQ // 2

    def other_head(p, carry):
        results = []
        for start in (0, half):
            length = start + half
            results.append(
                attend(q_buf[1 - head, p, start:length], keys_of(p, 0, length), keys_of(p, 1, length), start)
            )
        for start, rows in zip((0, half), results):
            out_ref[p, start : start + half, 0:HSIZE] = rows
            out_ref[p, start : start + half, HSIZE:] = rows
        return carry

    lax.fori_loop(0, PROMPTS_DEV, other_head, 0)

    for copy in first_copies():
        copy.wait_send()
    for ch in range(NY):
        twin_copy(ch, kv_buf.at[2 * ch + core]).wait_send()
    for i in range(4):
        near_copy(i, kv_buf.at[2 * handled(i) + core]).wait_send()

    for c, (start, length, batch) in enumerate(CHUNKS):
        size = length - start
        received = recv_bufs[c].at[pl.ds(1, NDP - 1)]
        pltpu.make_async_remote_copy(
            src_ref=received,
            dst_ref=received,
            send_sem=dp_send.at[c],
            recv_sem=dp_recv.at[c],
            device_id=(shifted(1, 1), tensor),
            device_id_type=MESH,
        ).wait()
        lower = jnp.full((size, HSIZE), head, jnp.int32) == 0

        def patch(p, carry):
            block = recv_bufs[c][slot_tab[p]]
            other = out_ref[p, start:length, 0:HSIZE]
            out_ref[p, start:length, 0:HSIZE] = jnp.where(lower, block, other)
            out_ref[p, start:length, HSIZE:] = jnp.where(lower, other, block)
            return carry

        lax.fori_loop(0, PROMPTS_DEV, patch, 0, unroll=2)


def on_device(queries, keys_values, donors, ablated):
    prompts, length, width = queries.shape
    pieces = keys_values.reshape(prompts, PIECE, 2, 4, HSIZE).transpose(3, 2, 0, 1, 4)
    anywhere = pl.BlockSpec(memory_space=pl.ANY)
    scalars = pl.BlockSpec(memory_space=pltpu.SMEM)
    dma = pltpu.SemaphoreType.DMA
    return pl.pallas_call(
        kernel,
        out_shape=jax.ShapeDtypeStruct(queries.shape, jnp.bfloat16),
        in_specs=[anywhere, pl.BlockSpec(memory_space=pltpu.VMEM), anywhere, scalars],
        out_specs=pl.BlockSpec(memory_space=pltpu.VMEM),
        scratch_shapes=[
            pltpu.VMEM((2, prompts, length, HSIZE), jnp.bfloat16),
            pltpu.VMEM((LAST, 2, prompts, PIECE, HSIZE), jnp.bfloat16),
            pltpu.VMEM((prompts, length, HSIZE), jnp.bfloat16),
            pltpu.VMEM((NDP * length, HSIZE), jnp.bfloat16),
            [pltpu.VMEM((NDP, last - start, HSIZE), jnp.bfloat16) for start, last, _ in CHUNKS],
            pltpu.SMEM(donors.shape[::-1], jnp.int32),
            pltpu.SMEM((NDP,), jnp.int32),
            pltpu.SMEM((PROMPTS_DEV,), jnp.int32),
            dma((2,)), dma, dma, dma((3,)), dma((4,)), dma((NY,)), dma((LAST,)), dma((len(CHUNKS),)), dma((len(CHUNKS),)),
        ],
        compiler_params=pltpu.CompilerParams(
            collective_id=0, has_side_effects=True, vmem_limit_bytes=40 * 2**20
        ),
    )(queries, pieces, donors.T, ablated)


def solution(mesh):
    return jax.shard_map(
        on_device,
        mesh=mesh,
        in_specs=(P("dp", None, "tensor"), P("dp", "tensor", None, None), P(), P()),
        out_specs=P("dp", None, "tensor"),
        check_vma=False,
    )
```

```python
import functools
import math

import jax
import jax.numpy as jnp
from jax import lax
from jax.experimental import pallas as pl
from jax.experimental.pallas import tpu as pltpu
from jax.sharding import PartitionSpec as P

MESH = pl.DeviceIdType.MESH
HSIZE = 128
PROMPTS_DEV = 16
SEQ = 256
NZ, NX, NY = 8, 4, 8
NDP = NZ * NX
PIECE = 16
CHIP = 2 * PIECE
CHUNKS = ((0, 64, 8), (64, 128, 4), (128, 256, 4))
WAVES = ((0, 4), (4, 8))
LAST = 2 * NY
RATE = math.log2(math.e) / math.sqrt(HSIZE)


def attend(query_rows, key_rows, value_rows, first):
    scores = lax.dot_general(
        query_rows, key_rows, (((1,), (1,)), ((), ())), preferred_element_type=jnp.float32
    )
    rows = lax.broadcasted_iota(jnp.int32, scores.shape, 0) + first
    columns = lax.broadcasted_iota(jnp.int32, scores.shape, 1)
    scores = jnp.where(rows >= columns, scores, -jnp.inf)
    row_max = jnp.max(scores, axis=1, keepdims=True)
    powers = jnp.exp2((scores - row_max) * RATE)
    weights = (powers * (1.0 / jnp.sum(powers, axis=1, keepdims=True))).astype(jnp.bfloat16)
    return jnp.dot(weights, value_rows, preferred_element_type=jnp.float32).astype(jnp.bfloat16)


def kernel(
    q_ref, kv_ref, donors_hbm, ablated_ref, out_ref,
    q_buf, kv_buf, own_buf, send_buf, recv_bufs, donors_ref, row_tab, slot_tab,
    q_sem, own_sem, table_sem, first_send, near_send, twin_send, kv_recv, dp_send, dp_recv,
):
    dp = lax.axis_index("dp")
    tensor = lax.axis_index("tensor")
    z, x = lax.div(dp, NX), lax.rem(dp, NX)
    y, core = lax.div(tensor, 2), lax.rem(tensor, 2)
    group = lax.div(y, 2)
    sign = 1 - 2 * lax.rem(y, 2)
    near = y + sign
    twin = 1 - core

    def in_group(chip, c):
        return (dp, lax.rem(chip + 2 * NY, NY) * 2 + c)

    def shifted(slot, direction):
        to_z = lax.rem(z + direction * lax.div(slot, NX) + NZ, NZ)
        to_x = lax.rem(x + direction * lax.rem(slot, NX) + NX, NX)
        return to_z * NX + to_x

    barrier = pltpu.get_barrier_semaphore()
    for target in [in_group(y - sign * i, core) for i in (1, 2, 3)] + [in_group(near, core), in_group(y, twin)]:
        pl.semaphore_signal(barrier, inc=1, device_id=target, device_id_type=MESH)

    def greet(slot, carry):
        pl.semaphore_signal(barrier, inc=1, device_id=(shifted(slot, -1), tensor), device_id_type=MESH)
        return carry

    lax.fori_loop(1, NDP, greet, 0)

    q_copies = [
        pltpu.make_async_copy(q_ref.at[:, :, pl.ds(i * HSIZE, HSIZE)], q_buf.at[i], q_sem.at[i])
        for i in range(2)
    ]
    for copy in q_copies:
        copy.start()
    own_copy = pltpu.make_async_copy(kv_ref.at[group], kv_buf.at[tensor], own_sem)
    own_copy.start()
    table_copy = pltpu.make_async_copy(donors_hbm, donors_ref, table_sem)
    table_copy.start()

    pl.semaphore_wait(barrier, NDP - 1 + 5)

    def forward(source, piece, part, sem, target):
        return pltpu.make_async_remote_copy(
            src_ref=source.at[part],
            dst_ref=kv_buf.at[piece, part],
            send_sem=sem,
            recv_sem=kv_recv.at[piece, part],
            device_id=target,
            device_id_type=MESH,
        )

    def first_copies(part):
        copies = []
        for i, step in enumerate((-1, 2, -3)):
            chip = lax.rem(y + sign * step + 2 * NY, NY)
            source = kv_ref.at[lax.div(chip, 2)]
            copies.append(forward(source, tensor, part, first_send.at[i, part], in_group(chip, core)))
        return copies

    def handled(i):
        return lax.rem(y - sign * i + 2 * NY, NY)

    def passed(i):
        return lax.rem(near + sign * i + 2 * NY, NY)

    def near_copy(i, source, part):
        return forward(source, 2 * handled(i) + core, part, near_send.at[i, part], in_group(near, core))

    def twin_copy(ch, source, part):
        return forward(source, 2 * ch + core, part, twin_send.at[ch, part], in_group(y, twin))

    def take(i, part):
        ch = handled(i)
        piece = kv_buf.at[2 * ch + core]
        near_copy(i, piece, part).wait_recv()
        near_copy(i, piece, part).start()
        twin_copy(ch, piece, part).start()

    def take_passed(i, part):
        ch = passed(i)
        piece = kv_buf.at[2 * ch + core]
        twin_copy(ch, piece, part).wait_recv()
        twin_copy(ch, piece, part).start()

    def when_in(chips, ch, action, *values):
        first, last = chips
        pl.when(jnp.logical_and(ch >= first, ch < last))(lambda: action(*values))

    def start_own():
        own = kv_ref.at[group]
        for part in range(2):
            for copy in [near_copy(0, own, part), twin_copy(y, own, part)] + first_copies(part):
                copy.start()

    def pass_on(chips):
        for part in range(2):
            when_in(chips, passed(0), take_passed, 0, part)
            for i in (1, 2, 3):
                when_in(chips, handled(i), take, i, part)
            for i in (1, 2, 3):
                when_in(chips, passed(i), take_passed, i, part)

    def arrive(chips):
        for ch in range(*chips):
            for part in range(2):
                piece = 2 * ch + twin
                forward(
                    kv_buf.at[piece], piece, part, twin_send.at[ch, part], in_group(y, twin)
                ).wait_recv()

    start_own()
    own_copy.wait()

    table_copy.wait()
    head = lax.rem(ablated_ref[tensor], 2)

    def find_row(slot, carry):
        dest = shifted(slot, 1)
        row = 0
        for p in range(PROMPTS_DEV):
            donor = donors_ref[tensor, dest * PROMPTS_DEV + p]
            row = row + jnp.where(lax.div(donor, PROMPTS_DEV) == dp, lax.rem(donor, PROMPTS_DEV), 0)
        row_tab[slot] = row
        return carry

    lax.fori_loop(0, NDP, find_row, 0)

    def find_slot(p, carry):
        source = lax.div(donors_ref[tensor, dp * PROMPTS_DEV + p], PROMPTS_DEV)
        slot_z = lax.rem(z - lax.div(source, NX) + NZ, NZ)
        slot_tab[p] = slot_z * NX + lax.rem(x - lax.rem(source, NX) + NX, NX)
        return carry

    lax.fori_loop(0, PROMPTS_DEV, find_slot, 0)

    def keys_of(p, part, length):
        return kv_buf[0 : length // PIECE, part, p].reshape(length, HSIZE)

    def ablated_chunk(start, length, batch):
        def prompts(i, carry):
            results = []
            for j in range(batch):
                p = i * batch + j
                results.append(
                    attend(q_buf[head, p, start:length], keys_of(p, 0, length), keys_of(p, 1, length), start)
                )
            for j in range(batch):
                own_buf[i * batch + j, start:length] = results[j]
            return carry

        lax.fori_loop(0, PROMPTS_DEV // batch, prompts, 0)

    def send_chunk(c, start, length):
        size = length - start
        recv_bufs[c][0] = own_buf[row_tab[0], start:length]

        def send(slot, carry):
            block = pl.ds(NDP * start + slot * size, size)
            send_buf[block] = own_buf[row_tab[slot], start:length]
            pltpu.make_async_remote_copy(
                src_ref=send_buf.at[block],
                dst_ref=recv_bufs[c].at[slot],
                send_sem=dp_send.at[c],
                recv_sem=dp_recv.at[c],
                device_id=(shifted(slot, 1), tensor),
                device_id_type=MESH,
            ).start()
            return carry

        lax.fori_loop(1, NDP, send, 0)

    for c, (start, length, batch) in enumerate(CHUNKS):
        wave = [w for w in range(len(WAVES)) if WAVES[w][0] * CHIP == start]
        for w in wave:
            pass_on(WAVES[w])
            arrive(WAVES[w])
        if c == 0:
            for copy in q_copies:
                copy.wait()
        ablated_chunk(start, length, batch)
        send_chunk(c, start, length)

    half = SEQ // 2

    def other_head(p, carry):
        results = []
        for start in (0, half):
            length = start + half
            results.append(
                attend(q_buf[1 - head, p, start:length], keys_of(p, 0, length), keys_of(p, 1, length), start)
            )
        for start, rows in zip((0, half), results):
            out_ref[p, start : start + half, 0:HSIZE] = rows
            out_ref[p, start : start + half, HSIZE:] = rows
        return carry

    lax.fori_loop(0, PROMPTS_DEV, other_head, 0)

    for part in range(2):
        for copy in first_copies(part):
            copy.wait_send()
        for ch in range(NY):
            twin_copy(ch, kv_buf.at[2 * ch + core], part).wait_send()
        for i in range(4):
            near_copy(i, kv_buf.at[2 * handled(i) + core], part).wait_send()

    for c, (start, length, batch) in enumerate(CHUNKS):
        size = length - start
        received = recv_bufs[c].at[pl.ds(1, NDP - 1)]
        pltpu.make_async_remote_copy(
            src_ref=received,
            dst_ref=received,
            send_sem=dp_send.at[c],
            recv_sem=dp_recv.at[c],
            device_id=(shifted(1, 1), tensor),
            device_id_type=MESH,
        ).wait()
        lower = jnp.full((size, HSIZE), head, jnp.int32) == 0

        def patch(p, carry):
            block = recv_bufs[c][slot_tab[p]]
            other = out_ref[p, start:length, 0:HSIZE]
            out_ref[p, start:length, 0:HSIZE] = jnp.where(lower, block, other)
            out_ref[p, start:length, HSIZE:] = jnp.where(lower, other, block)
            return carry

        lax.fori_loop(0, PROMPTS_DEV, patch, 0, unroll=2)


def on_device(queries, keys_values, donors, ablated):
    prompts, length, width = queries.shape
    pieces = keys_values.reshape(prompts, PIECE, 2, 4, HSIZE).transpose(3, 2, 0, 1, 4)
    anywhere = pl.BlockSpec(memory_space=pl.ANY)
    scalars = pl.BlockSpec(memory_space=pltpu.SMEM)
    dma = pltpu.SemaphoreType.DMA
    return pl.pallas_call(
        kernel,
        out_shape=jax.ShapeDtypeStruct(queries.shape, jnp.bfloat16),
        in_specs=[anywhere, pl.BlockSpec(memory_space=pltpu.VMEM), anywhere, scalars],
        out_specs=pl.BlockSpec(memory_space=pltpu.VMEM),
        scratch_shapes=[
            pltpu.VMEM((2, prompts, length, HSIZE), jnp.bfloat16),
            pltpu.VMEM((LAST, 2, prompts, PIECE, HSIZE), jnp.bfloat16),
            pltpu.VMEM((prompts, length, HSIZE), jnp.bfloat16),
            pltpu.VMEM((NDP * length, HSIZE), jnp.bfloat16),
            [pltpu.VMEM((NDP, last - start, HSIZE), jnp.bfloat16) for start, last, _ in CHUNKS],
            pltpu.SMEM(donors.shape[::-1], jnp.int32),
            pltpu.SMEM((NDP,), jnp.int32),
            pltpu.SMEM((PROMPTS_DEV,), jnp.int32),
            dma((2,)), dma, dma, dma((3, 2)), dma((4, 2)), dma((NY, 2)), dma((LAST, 2)), dma((len(CHUNKS),)), dma((len(CHUNKS),)),
        ],
        compiler_params=pltpu.CompilerParams(
            collective_id=0, has_side_effects=True, vmem_limit_bytes=40 * 2**20
        ),
    )(queries, pieces, donors.T, ablated)


def solution(mesh):
    return jax.shard_map(
        on_device,
        mesh=mesh,
        in_specs=(P("dp", None, "tensor"), P("dp", "tensor", None, None), P(), P()),
        out_specs=P("dp", None, "tensor"),
        check_vma=False,
    )
```

```python
import functools
import math

import jax
import jax.numpy as jnp
from jax import lax
from jax.experimental import pallas as pl
from jax.experimental.pallas import tpu as pltpu
from jax.sharding import PartitionSpec as P

MESH = pl.DeviceIdType.MESH
HSIZE = 128
PROMPTS_DEV = 16
SEQ = 256
NZ, NX, NY = 8, 4, 8
NDP = NZ * NX
PIECE = 16
CHIP = 2 * PIECE
CHUNKS = ((0, 64, 8), (64, 128, 8), (128, 256, 4))
WAVES = ((0, 4), (4, 8))
LAST = 2 * NY
RATE = math.log2(math.e) / math.sqrt(HSIZE)


def attend(query_rows, key_rows, value_rows, first):
    scores = lax.dot_general(
        query_rows, key_rows, (((1,), (1,)), ((), ())), preferred_element_type=jnp.float32
    )
    rows = lax.broadcasted_iota(jnp.int32, scores.shape, 0) + first
    columns = lax.broadcasted_iota(jnp.int32, scores.shape, 1)
    scores = jnp.where(rows >= columns, scores, -jnp.inf)
    row_max = jnp.max(scores, axis=1, keepdims=True)
    powers = jnp.exp2((scores - row_max) * RATE)
    weights = (powers * (1.0 / jnp.sum(powers, axis=1, keepdims=True))).astype(jnp.bfloat16)
    return jnp.dot(weights, value_rows, preferred_element_type=jnp.float32).astype(jnp.bfloat16)


def kernel(
    q_ref, kv_ref, donors_hbm, ablated_ref, out_ref,
    q_buf, kv_buf, own_buf, send_buf, recv_bufs, donors_ref, row_tab, slot_tab,
    q_sem, own_sem, table_sem, first_send, near_send, twin_send, kv_recv, dp_send, dp_recv,
):
    dp = lax.axis_index("dp")
    tensor = lax.axis_index("tensor")
    z, x = lax.div(dp, NX), lax.rem(dp, NX)
    y, core = lax.div(tensor, 2), lax.rem(tensor, 2)
    group = lax.div(y, 2)
    sign = 1 - 2 * lax.rem(y, 2)
    near = y + sign
    twin = 1 - core

    def in_group(chip, c):
        return (dp, lax.rem(chip + 2 * NY, NY) * 2 + c)

    def shifted(slot, direction):
        to_z = lax.rem(z + direction * lax.div(slot, NX) + NZ, NZ)
        to_x = lax.rem(x + direction * lax.rem(slot, NX) + NX, NX)
        return to_z * NX + to_x

    barrier = pltpu.get_barrier_semaphore()
    for target in [in_group(y - sign * i, core) for i in (1, 2, 3)] + [in_group(near, core), in_group(y, twin)]:
        pl.semaphore_signal(barrier, inc=1, device_id=target, device_id_type=MESH)

    def greet(slot, carry):
        pl.semaphore_signal(barrier, inc=1, device_id=(shifted(slot, -1), tensor), device_id_type=MESH)
        return carry

    lax.fori_loop(1, NDP, greet, 0)

    q_copies = [
        pltpu.make_async_copy(q_ref.at[:, :, pl.ds(i * HSIZE, HSIZE)], q_buf.at[i], q_sem.at[i])
        for i in range(2)
    ]
    for copy in q_copies:
        copy.start()
    own_copy = pltpu.make_async_copy(kv_ref.at[group], kv_buf.at[tensor], own_sem)
    own_copy.start()
    table_copy = pltpu.make_async_copy(donors_hbm, donors_ref, table_sem)
    table_copy.start()

    pl.semaphore_wait(barrier, NDP - 1 + 5)

    def forward(source, piece, part, sem, target):
        return pltpu.make_async_remote_copy(
            src_ref=source.at[part],
            dst_ref=kv_buf.at[piece, part],
            send_sem=sem,
            recv_sem=kv_recv.at[piece, part],
            device_id=target,
            device_id_type=MESH,
        )

    def first_copies(part):
        copies = []
        for i, step in enumerate((-1, 2, -3)):
            chip = lax.rem(y + sign * step + 2 * NY, NY)
            source = kv_ref.at[lax.div(chip, 2)]
            copies.append(forward(source, tensor, part, first_send.at[i, part], in_group(chip, core)))
        return copies

    def handled(i):
        return lax.rem(y - sign * i + 2 * NY, NY)

    def passed(i):
        return lax.rem(near + sign * i + 2 * NY, NY)

    def near_copy(i, source, part):
        return forward(source, 2 * handled(i) + core, part, near_send.at[i, part], in_group(near, core))

    def twin_copy(ch, source, part):
        return forward(source, 2 * ch + core, part, twin_send.at[ch, part], in_group(y, twin))

    def take(i, part):
        ch = handled(i)
        piece = kv_buf.at[2 * ch + core]
        near_copy(i, piece, part).wait_recv()
        near_copy(i, piece, part).start()
        twin_copy(ch, piece, part).start()

    def take_passed(i, part):
        ch = passed(i)
        piece = kv_buf.at[2 * ch + core]
        twin_copy(ch, piece, part).wait_recv()
        twin_copy(ch, piece, part).start()

    def when_in(chips, ch, action, *values):
        first, last = chips
        pl.when(jnp.logical_and(ch >= first, ch < last))(lambda: action(*values))

    def start_own():
        own = kv_ref.at[group]
        for part in range(2):
            for copy in [near_copy(0, own, part), twin_copy(y, own, part)] + first_copies(part):
                copy.start()

    def pass_on(chips):
        for part in range(2):
            when_in(chips, passed(0), take_passed, 0, part)
            for i in (1, 2, 3):
                when_in(chips, handled(i), take, i, part)
            for i in (1, 2, 3):
                when_in(chips, passed(i), take_passed, i, part)

    def arrive(chips):
        for ch in range(*chips):
            for part in range(2):
                piece = 2 * ch + twin
                forward(
                    kv_buf.at[piece], piece, part, twin_send.at[ch, part], in_group(y, twin)
                ).wait_recv()

    start_own()
    own_copy.wait()

    table_copy.wait()
    head = lax.rem(ablated_ref[tensor], 2)

    def find_row(slot, carry):
        dest = shifted(slot, 1)
        row = 0
        for p in range(PROMPTS_DEV):
            donor = donors_ref[tensor, dest * PROMPTS_DEV + p]
            row = row + jnp.where(lax.div(donor, PROMPTS_DEV) == dp, lax.rem(donor, PROMPTS_DEV), 0)
        row_tab[slot] = row
        return carry

    lax.fori_loop(0, NDP, find_row, 0)

    def find_slot(p, carry):
        source = lax.div(donors_ref[tensor, dp * PROMPTS_DEV + p], PROMPTS_DEV)
        slot_z = lax.rem(z - lax.div(source, NX) + NZ, NZ)
        slot_tab[p] = slot_z * NX + lax.rem(x - lax.rem(source, NX) + NX, NX)
        return carry

    lax.fori_loop(0, PROMPTS_DEV, find_slot, 0)

    def keys_of(p, part, length):
        return kv_buf[0 : length // PIECE, part, p].reshape(length, HSIZE)

    def ablated_chunk(start, length, batch):
        def prompts(i, carry):
            results = []
            for j in range(batch):
                p = i * batch + j
                results.append(
                    attend(q_buf[head, p, start:length], keys_of(p, 0, length), keys_of(p, 1, length), start)
                )
            for j in range(batch):
                own_buf[i * batch + j, start:length] = results[j]
            return carry

        lax.fori_loop(0, PROMPTS_DEV // batch, prompts, 0)

    def send_chunk(c, start, length):
        size = length - start
        recv_bufs[c][0] = own_buf[row_tab[0], start:length]

        def send(slot, carry):
            block = pl.ds(NDP * start + slot * size, size)
            send_buf[block] = own_buf[row_tab[slot], start:length]
            pltpu.make_async_remote_copy(
                src_ref=send_buf.at[block],
                dst_ref=recv_bufs[c].at[slot],
                send_sem=dp_send.at[c],
                recv_sem=dp_recv.at[c],
                device_id=(shifted(slot, 1), tensor),
                device_id_type=MESH,
            ).start()
            return carry

        lax.fori_loop(1, NDP, send, 0)

    for c, (start, length, batch) in enumerate(CHUNKS):
        wave = [w for w in range(len(WAVES)) if WAVES[w][0] * CHIP == start]
        for w in wave:
            pass_on(WAVES[w])
        arrive((start // CHIP, length // CHIP))
        if c == 0:
            for copy in q_copies:
                copy.wait()
        ablated_chunk(start, length, batch)
        send_chunk(c, start, length)

    half = SEQ // 2

    def other_head(p, carry):
        results = []
        for start in (0, half):
            length = start + half
            results.append(
                attend(q_buf[1 - head, p, start:length], keys_of(p, 0, length), keys_of(p, 1, length), start)
            )
        for start, rows in zip((0, half), results):
            out_ref[p, start : start + half, 0:HSIZE] = rows
            out_ref[p, start : start + half, HSIZE:] = rows
        return carry

    lax.fori_loop(0, PROMPTS_DEV, other_head, 0)

    for part in range(2):
        for copy in first_copies(part):
            copy.wait_send()
        for ch in range(NY):
            twin_copy(ch, kv_buf.at[2 * ch + core], part).wait_send()
        for i in range(4):
            near_copy(i, kv_buf.at[2 * handled(i) + core], part).wait_send()

    for c, (start, length, batch) in enumerate(CHUNKS):
        size = length - start
        received = recv_bufs[c].at[pl.ds(1, NDP - 1)]
        pltpu.make_async_remote_copy(
            src_ref=received,
            dst_ref=received,
            send_sem=dp_send.at[c],
            recv_sem=dp_recv.at[c],
            device_id=(shifted(1, 1), tensor),
            device_id_type=MESH,
        ).wait()
        lower = jnp.full((size, HSIZE), head, jnp.int32) == 0

        def patch(p, carry):
            block = recv_bufs[c][slot_tab[p]]
            other = out_ref[p, start:length, 0:HSIZE]
            out_ref[p, start:length, 0:HSIZE] = jnp.where(lower, block, other)
            out_ref[p, start:length, HSIZE:] = jnp.where(lower, other, block)
            return carry

        lax.fori_loop(0, PROMPTS_DEV, patch, 0, unroll=2)


def on_device(queries, keys_values, donors, ablated):
    prompts, length, width = queries.shape
    pieces = keys_values.reshape(prompts, PIECE, 2, 4, HSIZE).transpose(3, 2, 0, 1, 4)
    anywhere = pl.BlockSpec(memory_space=pl.ANY)
    scalars = pl.BlockSpec(memory_space=pltpu.SMEM)
    dma = pltpu.SemaphoreType.DMA
    return pl.pallas_call(
        kernel,
        out_shape=jax.ShapeDtypeStruct(queries.shape, jnp.bfloat16),
        in_specs=[anywhere, pl.BlockSpec(memory_space=pltpu.VMEM), anywhere, scalars],
        out_specs=pl.BlockSpec(memory_space=pltpu.VMEM),
        scratch_shapes=[
            pltpu.VMEM((2, prompts, length, HSIZE), jnp.bfloat16),
            pltpu.VMEM((LAST, 2, prompts, PIECE, HSIZE), jnp.bfloat16),
            pltpu.VMEM((prompts, length, HSIZE), jnp.bfloat16),
            pltpu.VMEM((NDP * length, HSIZE), jnp.bfloat16),
            [pltpu.VMEM((NDP, last - start, HSIZE), jnp.bfloat16) for start, last, _ in CHUNKS],
            pltpu.SMEM(donors.shape[::-1], jnp.int32),
            pltpu.SMEM((NDP,), jnp.int32),
            pltpu.SMEM((PROMPTS_DEV,), jnp.int32),
            dma((2,)), dma, dma, dma((3, 2)), dma((4, 2)), dma((NY, 2)), dma((LAST, 2)), dma((len(CHUNKS),)), dma((len(CHUNKS),)),
        ],
        compiler_params=pltpu.CompilerParams(
            collective_id=0, has_side_effects=True, vmem_limit_bytes=60 * 2**20
        ),
    )(queries, pieces, donors.T, ablated)


def solution(mesh):
    return jax.shard_map(
        on_device,
        mesh=mesh,
        in_specs=(P("dp", None, "tensor"), P("dp", "tensor", None, None), P(), P()),
        out_specs=P("dp", None, "tensor"),
        check_vma=False,
    )
```
